32 devices in a mesh: pb: 4 (over y, x), pa: 4 (over z), ma: 2 (over core).
Axes of the slice: x: 2, y: 2, z: 4, core: 2. Of those that a mesh axis runs over, the one named last changes fastest.
Arguments:
- encoded: bfloat16 [4, 8, 256, 4096], P('pb', 'pa'), may hold values from -6 to 6
- key_weight: bfloat16 [4096, 2048], P('pa', 'ma'), may hold values from -0.09375 to 0.09375
- value_weight: bfloat16 [4096, 2048], P('pa', 'ma'), may hold values from -0.09375 to 0.09375
- queries: bfloat16 [4, 32, 2048], P('pb', None, 'ma')
- key_len: int32 [4, 8], P('pb', 'pa'), may hold values from 64 to 256, as said below
- retr_query: float32 [4, 768], P('pb')
- passage_ids: int32 [4, 8], P('pb'), may hold values from 0 to 3
- placement_perm: int32 [4, 4], P('pb'), may hold values from 0 to 3, each once within a row
- pool_in: bfloat16 [16, 256, 768], P(('pb', 'pa')), may hold values from -6 to 6
- pool_pre: bfloat16 [16, 256, 768], P(('pb', 'pa')), may hold values from -6 to 6
- pool_len: int32 [16], P(('pb', 'pa')), may hold values from 64 to 256, as said below
- up_weight: bfloat16 [768, 3072], P(None, 'ma'), may hold values from -0.21875 to 0.21875
- up_bias: float32 [3072], P('ma'), may hold values from -3 to 3
- down_weight: bfloat16 [768, 3072], P(None, 'ma'), may hold values from -0.109375 to 0.109375
- norm_gain: float32 [768], replicated, may hold values from 0.1 to 1.9
Outputs:
- attn_out: bfloat16 [4, 32, 2048], P('pb', None, 'ma')
- pool_grad: bfloat16 [16, 256, 768], P(('pb', 'pa'))
- up_grad: float32 [768, 3072], P(('pb', 'pa'), 'ma')
- down_grad: float32 [768, 3072], P(('pb', 'pa'), 'ma')
The draws below stay inside these ranges and needn't reach their ends.
Inputs may be any that keep to these rules, and one draw needn't show every extreme that they name: `key_len`: at least one passage of every question has 256 tokens. `pool_len`: at least one pool passage has 256 tokens. `passage_ids`: indices into the pool of the question's own group; several reads may name the same pool passage. Each row is a permutation: pool passage k of group g is stored at position g * 4 + placement_perm[g, k].
All inputs are finite; a program needn't handle non-finite values.
Results may differ from the reference program's by a relative error of at most 0.0049.
Values may be sent and summed in bfloat16 or wider, within the bound.
No kernel may reach another device: no remote copies, remote signals or barrier semaphores. Data moves between devices by JAX's collectives and lax.ppermute only.
A program may use at most 128 MiB of HBM per device.

```python
import math
import jax
import jax.numpy as jnp
import numpy as np
from jax import lax

D = 4096
HEADS = 32
HDIM = 64
ANS = 32
PLEN = 256
DR = 768
FF = 3072
Q_DEV = 1
BATCH = 4
PASSAGES = 8
GROUP_POOL = 4
GROUPS = 4
POOL = 16
HEAD_COLS = 2048


def draw_queries(key, part):
    base = jax.random.normal(jax.random.fold_in(key, 11), (BATCH, ANS, HEAD_COLS), jnp.float32) * 0.25
    return base.astype(jnp.bfloat16)


def draw_retr_query(key, part):
    base = jax.random.normal(jax.random.fold_in(key, 21), (BATCH, DR), jnp.float32) * 0.3
    return base


def draw_key_len(key, part):
    lengths = jax.random.randint(jax.random.fold_in(key, 31), (BATCH, PASSAGES), PLEN // 4, PLEN + 1, jnp.int32)
    return lengths.at[:, 0].set(PLEN).at[:, 1].set(PLEN // 4)


def draw_pool_len(key, part):
    lengths = jax.random.randint(jax.random.fold_in(key, 41), (POOL,), PLEN // 4, PLEN + 1, jnp.int32)
    return lengths.at[0].set(PLEN).at[1].set(PLEN // 4)


def plant(values, key, low, top_value):
    longest = values.shape.index(max(values.shape))
    spots = []
    for shift in (0, 1):
        where = [jax.random.randint(jax.random.fold_in(key, axis), (), 0, length) for axis, length in enumerate(values.shape)]
        where[longest] = (where[longest] + shift) % values.shape[longest]
        spots.append(tuple(where))
    return values.at[spots[0]].set(low).at[spots[1]].set(top_value)


def shard_levels(stream_key, shape, pieces, smallest, high):
    loudness = 1.0
    for position, parts in pieces:
        draws = jax.random.uniform(jax.random.fold_in(jax.random.fold_in(stream_key, 6), position), (parts,), jnp.float32, smallest / len(pieces), high / len(pieces))
        loudness = loudness * jnp.repeat(jnp.exp(draws), shape[position] // parts).reshape((-1,) + (1,) * (len(shape) - 1 - position))
    return loudness


def rank_bounds(count, lean):
    loads = [(1 << 20) // math.isqrt(standing ** lean) + 1 for standing in range(1, count + 1)]
    deviation = 1 + sum(loads) // (1 << 30)
    return np.cumsum(np.array([max(1, weight // deviation) for weight in loads]))


def ranked(rng, shape, amount, skew):
    grid = rank_bounds(amount, skew)
    pick = jax.random.randint(jax.random.fold_in(rng, 1), shape, 0, int(grid[amount - 1]))
    standing = jnp.searchsorted(jnp.asarray(grid, jnp.int32), pick, side="right")
    return jax.random.permutation(jax.random.fold_in(rng, 2), amount)[standing].astype(jnp.int32)


def noise(stream_key, extent, deviation, bound, cuts=(), held_as=jnp.bfloat16):
    values = deviation * jax.random.normal(stream_key, extent, jnp.float32)
    if cuts:
        values = values * shard_levels(stream_key, extent, cuts, -0.22, 0.18)
    return jnp.clip(values, -bound, bound).astype(held_as)


def setup_inputs(seed: int = 0) -> dict:
    streams_of = jax.random.split(jax.random.key(seed), 16)
    return {
        "encoded": noise(streams_of[0], (BATCH, PASSAGES, PLEN, D), 1.0, 6.0, ((0, 4), (1, 4))),
        "key_weight": noise(streams_of[1], (D, HEAD_COLS), D ** -0.5, 0.09375, ((0, 4), (1, 2))),
        "value_weight": noise(streams_of[2], (D, HEAD_COLS), D ** -0.5, 0.09375, ((0, 4), (1, 2))),
        "queries": draw_queries(jax.random.fold_in(streams_of[15], 71), 0),
        "key_len": draw_key_len(jax.random.fold_in(streams_of[15], 71), 0),
        "retr_query": draw_retr_query(jax.random.fold_in(streams_of[15], 71), 0),
        "passage_ids": plant(ranked(streams_of[6], (BATCH, PASSAGES), GROUP_POOL, 0), jax.random.fold_in(streams_of[6], 3), 0, GROUP_POOL - 1).astype(jnp.int32),
        "placement_perm": jax.vmap(lambda own: jax.random.permutation(own, GROUP_POOL))(jax.random.split(streams_of[7], GROUPS)).reshape((GROUPS, GROUP_POOL)).astype(jnp.int32),
        "pool_in": noise(streams_of[8], (POOL, PLEN, DR), 1.0, 6.0, ((0, 16),)),
        "pool_pre": noise(streams_of[9], (POOL, PLEN, DR), 1.0, 6.0, ((0, 16),)),
        "pool_len": draw_pool_len(jax.random.fold_in(streams_of[15], 71), 0),
        "up_weight": noise(streams_of[11], (DR, FF), DR ** -0.5, 0.21875, ((1, 2),)),
        "up_bias": noise(streams_of[12], (FF,), 0.5, 3.0, ((0, 2),), jnp.float32),
        "down_weight": noise(streams_of[13], (DR, FF), FF ** -0.5, 0.109375, ((1, 2),)),
        "norm_gain": jnp.clip(1.0 + 0.18 * jax.random.normal(streams_of[14], (DR,), jnp.float32), 0.1, 1.9),
    }


loss_scale = 16384.0
highest = lax.Precision.HIGHEST

def gelu_exact(upper):
    return 0.5 * upper * (1.0 + lax.erf(upper * 0.7071067811865476))

def gelu_slope(upper):
    return 0.5 * (1.0 + lax.erf(upper * 0.7071067811865476)) + upper * jnp.exp(-0.5 * upper * upper) * 0.3989422804014327

def reference(encoded, key_weight, value_weight, queries, key_len, retr_query, passage_ids, placement_perm, pool_in, pool_pre, pool_len, up_weight, up_bias, down_weight, norm_gain):

    def reader_one(items):
        enc_one, query_one, len_one = items

        def project(enc_pass):
            return (jnp.dot(enc_pass, key_weight, preferred_element_type=jnp.float32), jnp.dot(enc_pass, value_weight, preferred_element_type=jnp.float32))
        keys, values = lax.map(project, enc_one)
        keys = keys.reshape(PASSAGES * PLEN, HEADS, HDIM)
        values = values.reshape(PASSAGES * PLEN, HEADS, HDIM)
        query_f = query_one.astype(jnp.float32).reshape(ANS, HEADS, HDIM)
        scores = jnp.einsum('ahj,thj->aht', query_f, keys, precision=highest)
        valid = (jnp.arange(PLEN)[None, :] < len_one[:, None]).reshape(PASSAGES * PLEN)
        masked = jnp.where(valid, scores, -1e+30)
        largest = lax.optimization_barrier(jnp.max(masked, axis=-1))
        weights = jnp.where(valid, jnp.exp(masked - largest[..., None]), 0.0)
        totals = lax.optimization_barrier(jnp.sum(weights, axis=-1))
        summed = jnp.einsum('aht,thj->ahj', weights, values, precision=highest)
        output = (summed / totals[..., None]).astype(jnp.bfloat16).reshape(ANS, HEAD_COLS)
        shares = (weights / totals[..., None]).reshape(ANS, HEADS, PASSAGES, PLEN)
        mass_one = lax.optimization_barrier(jnp.sum(shares, axis=(0, 1, 3))) / (ANS * HEADS)
        return (output, mass_one)
    attn_out, mass = lax.map(reader_one, (encoded, queries, key_len))
    pre_f = pool_pre.astype(jnp.float32)
    centre = pre_f - lax.optimization_barrier(jnp.mean(pre_f, axis=-1, keepdims=True))
    spread = lax.optimization_barrier(jnp.mean(centre * centre, axis=-1, keepdims=True))
    inverse = 1.0 / jnp.sqrt(spread + 1e-05)
    normed = centre * inverse
    live = (jnp.arange(PLEN)[None, :] < pool_len[:, None]).astype(jnp.float32)
    lengths = pool_len.astype(jnp.float32)
    embed = lax.optimization_barrier(jnp.sum(normed * norm_gain * live[..., None], axis=1)) / lengths[:, None]
    group = (jnp.arange(BATCH) // Q_DEV).astype(jnp.int32)
    where_at = group[:, None] * GROUP_POOL + placement_perm[group[:, None], passage_ids]
    chosen = embed[where_at]
    sim = jnp.einsum('bd,bpd->bp', retr_query, chosen, precision=highest)
    p_ret = jax.nn.softmax(sim, axis=-1)
    coef = loss_scale * (p_ret - mass)
    terms = (coef[..., None] * retr_query[:, None, :]).reshape(BATCH * PASSAGES, DR)
    signal = jax.ops.segment_sum(terms, where_at.reshape(-1), num_segments=POOL)
    dnorm = signal[:, None, :] * live[..., None] * norm_gain / lengths[:, None, None]
    dpre = (dnorm - lax.optimization_barrier(jnp.mean(dnorm, axis=-1, keepdims=True)) - normed * lax.optimization_barrier(jnp.mean(dnorm * normed, axis=-1, keepdims=True))) * inverse

    def backward_one(carry, items):
        input_one, dpre_one = items
        dpre_b = dpre_one.astype(jnp.bfloat16)
        upper = jnp.dot(input_one, up_weight, preferred_element_type=jnp.float32) + up_bias
        act_b = gelu_exact(upper).astype(jnp.bfloat16)
        dact = jnp.dot(dpre_b, down_weight, preferred_element_type=jnp.float32)
        dup_b = (dact * gelu_slope(upper)).astype(jnp.bfloat16)
        grad_up = carry[0] + jnp.dot(input_one.T, dup_b, preferred_element_type=jnp.float32)
        grad_down = carry[1] + jnp.dot(dpre_b.T, act_b, preferred_element_type=jnp.float32)
        back = jnp.dot(dup_b, up_weight.T, preferred_element_type=jnp.float32)
        return ((grad_up, grad_down), (dpre_one + back).astype(jnp.bfloat16))
    start = (jnp.zeros((DR, FF), jnp.float32), jnp.zeros((DR, FF), jnp.float32))
    (up_grad, down_grad), pool_grad = lax.scan(backward_one, start, (pool_in, dpre))
    return (attn_out, pool_grad, up_grad, down_grad)
```

```python
import jax
import jax.numpy as jnp
from jax import lax
from jax.experimental import pallas as pl
from jax.experimental.pallas import tpu as pltpu
from jax.sharding import PartitionSpec as P

HEADS = 32
HDIM = 64
ANS = 32
DR = 768


RING_MOST = 4


loss_scale = 16384.0
highest = lax.Precision.HIGHEST


def gelu_exact(upper):
    return 0.5 * upper * (1.0 + lax.erf(upper * 0.7071067811865476))


def gelu_slope(upper):
    return (
        0.5 * (1.0 + lax.erf(upper * 0.7071067811865476))
        + upper * jnp.exp(-0.5 * upper * upper) * 0.3989422804014327
    )


def ring_order(count):
    return list(range(0, count, 2)) + [i for i in range(count - 1, 0, -1) if i % 2]


def ring_next(count):
    order = ring_order(count)
    return [(order[i], order[(i + 1) % count]) for i in range(count)]


def flip(values, bit):
    count = lax.axis_size("pb")
    return lax.ppermute(values, "pb", [(i, i ^ bit) for i in range(count)])


def after(value, *others):
    return lax.optimization_barrier((value,) + others)[0]


def plane_gather(piece, through):
    from_x = flip(piece, 1)
    from_y = flip(piece, 2)
    far = flip(from_y, 1) if through == 1 else flip(from_x, 2)
    return [piece, from_x, from_y, far]


COLUMNS = 256


def accumulate(refs, has_total, counts):
    at = 0
    total = None
    if has_total:
        total = refs[0][...]
        at = 1
    for count in counts:
        rows, parts = refs[at], refs[at + 1 : at + 1 + count]
        at += 1 + count
        start = 0
        for part in parts:
            stop = start + part.shape[0]
            term = jnp.dot(rows[:, start:stop], part[...], preferred_element_type=jnp.float32)
            total = term if total is None else total + term
            start = stop
    return total, refs[at:]


def two_terms(values):
    high = values.astype(jnp.bfloat16)
    return high, (values - high.astype(jnp.float32)).astype(jnp.bfloat16)


def projection(total, groups, finish, extra, extra_specs, out_shape, out_specs):
    arrays = [] if total is None else [total]
    wide = lambda count: pl.BlockSpec((count, COLUMNS), lambda i: (0, i))
    specs = [] if total is None else [wide(total.shape[0])]
    flops = 0
    for rows, parts in groups:
        arrays += [rows] + list(parts)
        specs += [pl.BlockSpec(rows.shape, lambda i: (0, 0))] + [wide(part.shape[0]) for part in parts]
        flops += 2 * rows.shape[0] * rows.shape[1] * parts[0].shape[1]
    counts = [len(parts) for _, parts in groups]

    def kernel(*refs):
        value, rest = accumulate(refs, total is not None, counts)
        finish(value, *rest)

    return pl.pallas_call(
        kernel,
        grid=(groups[0][1][0].shape[1] // COLUMNS,),
        in_specs=specs + list(extra_specs),
        out_specs=out_specs,
        out_shape=out_shape,
        compiler_params=pltpu.CompilerParams(vmem_limit_bytes=32 << 20),
        cost_estimate=pl.CostEstimate(flops=flops, bytes_accessed=8 << 20, transcendentals=0),
    )(*arrays, *extra)


def store(value, out_ref):
    out_ref[...] = value


def running(total, groups):
    tokens, columns = groups[0][0].shape[0], groups[0][1][0].shape[1]
    return projection(
        total,
        groups,
        store,
        (),
        (),
        jax.ShapeDtypeStruct((tokens, columns), jnp.float32),
        pl.BlockSpec((tokens, COLUMNS), lambda i: (0, i)),
    )


def scores_of(total, groups, query_blocks, valid, p_here):
    tokens = groups[0][0].shape[0]
    pairs = query_blocks.shape[1]
    blocks = groups[0][1][0].shape[1] // COLUMNS
    each = tokens // p_here

    def finish(keys, query_ref, valid_ref, weight_ref, stat_ref):
        high, low = two_terms(keys)
        query = query_ref[...]
        scores = jnp.dot(high, query, preferred_element_type=jnp.float32)
        scores = scores + jnp.dot(low, query, preferred_element_type=jnp.float32)
        alive = valid_ref[...] > 0.0
        scores = jnp.where(alive, scores, -1e30)
        top = jnp.max(scores, axis=0, keepdims=True)
        weights = jnp.where(alive, jnp.exp(scores - top), 0.0)
        weight_ref[...] = weights
        rows = [top] + [
            jnp.sum(weights[p * each : (p + 1) * each], axis=0, keepdims=True) for p in range(p_here)
        ]
        for i, row in enumerate(rows):
            stat_ref[i : i + 1, :] = row

    wide = pairs // blocks
    return projection(
        total,
        groups,
        finish,
        (query_blocks, valid),
        (
            pl.BlockSpec((COLUMNS, wide), lambda i: (0, i)),
            pl.BlockSpec((tokens, wide), lambda i: (0, 0)),
        ),
        (
            jax.ShapeDtypeStruct((tokens, pairs), jnp.float32),
            jax.ShapeDtypeStruct((1 + p_here, pairs), jnp.float32),
        ),
        (
            pl.BlockSpec((tokens, wide), lambda i: (0, i)),
            pl.BlockSpec((1 + p_here, wide), lambda i: (0, i)),
        ),
    )


def summed_of(total, groups, weights, ratio):
    tokens, pairs = weights.shape
    columns = groups[0][1][0].shape[1]
    blocks = columns // COLUMNS
    wide = pairs // blocks

    def finish(values, weight_ref, ratio_ref, out_ref):
        high, low = two_terms(values)
        w_high, w_low = two_terms(weight_ref[...] * ratio_ref[...])
        over = (((0,), (0,)), ((), ()))
        full = lax.dot_general(w_high, high, over, preferred_element_type=jnp.float32)
        full = full + lax.dot_general(w_high, low, over, preferred_element_type=jnp.float32)
        full = full + lax.dot_general(w_low, high, over, preferred_element_type=jnp.float32)
        head = lax.broadcasted_iota(jnp.int32, (ANS, COLUMNS), 1) // HDIM
        out = jnp.zeros((ANS, COLUMNS), jnp.float32)
        for h in range(COLUMNS // HDIM):
            out = jnp.where(head == h, full[h * ANS : (h + 1) * ANS], out)
        out_ref[...] = out

    return projection(
        total,
        groups,
        finish,
        (weights, ratio),
        (
            pl.BlockSpec((tokens, wide), lambda i: (0, i)),
            pl.BlockSpec((1, wide), lambda i: (0, i)),
        ),
        jax.ShapeDtypeStruct((ANS, columns), jnp.float32),
        pl.BlockSpec((ANS, COLUMNS), lambda i: (0, i)),
    )


def quarter_of(weight):
    quarter = weight.shape[0] // lax.axis_size("pb")
    return lax.dynamic_slice_in_dim(weight, lax.axis_index("pb") * quarter, quarter, 0)


def ring_step(piece):
    return lax.ppermute(piece, "pa", ring_next(lax.axis_size("pa")))


def local(
    encoded,
    key_weight,
    value_weight,
    queries,
    key_len,
    retr_query,
    passage_ids,
    placement_perm,
    pool_in,
    pool_pre,
    pool_len,
    up_weight,
    up_bias,
    down_weight,
    norm_gain,
):
    q_here, p_here, tokens, width = encoded.shape
    pb_count = lax.axis_size("pb")
    pa_count = lax.axis_size("pa")
    ma_count = lax.axis_size("ma")
    pb_at = lax.axis_index("pb")
    pa_at = lax.axis_index("pa")
    ma_at = lax.axis_index("ma")
    heads_here = HEADS // ma_count
    cols_here = key_weight.shape[1]
    depth = key_weight.shape[0]
    token_rows = encoded.reshape(p_here * tokens, width)

    order = jnp.array(ring_order(pa_count), jnp.int32)
    place = jnp.argmax(order == pa_at).astype(jnp.int32)

    def columns_of(step, quarter):
        owner = order[(place - step + pa_count) % pa_count]
        if quarter is None:
            return lax.dynamic_slice_in_dim(token_rows, owner * depth, depth, 1)
        return jnp.concatenate(
            [
                lax.dynamic_slice_in_dim(token_rows, owner * depth + (pb_at ^ q) * quarter, quarter, 1)
                for q in range(pb_count)
            ],
            axis=1,
        )

    positions = jnp.arange(tokens, dtype=jnp.int32)
    grouped = pa_count <= RING_MOST
    rows = DR // (pb_count * pa_count)
    ff_here = up_weight.shape[1]
    ma_flip = [(i, ma_count - 1 - i) for i in range(ma_count)]
    blocks = cols_here // COLUMNS
    in_block = COLUMNS // HDIM
    pairs = ANS * heads_here
    same = jnp.eye(in_block, dtype=jnp.bfloat16)
    query_blocks = jnp.einsum(
        "abgj,gh->gjbha", queries[0].reshape(ANS, blocks, in_block, HDIM), same
    ).reshape(COLUMNS, pairs)
    valid = (positions[None, :] < key_len[0][:, None]).astype(jnp.float32).reshape(-1, 1)
    valid = jnp.broadcast_to(valid, (p_here * tokens, pairs // blocks))
    if grouped:
        quarter = depth // pb_count
        own_rows = columns_of(0, None)
        other_rows = [columns_of(step, quarter) for step in range(1, pa_count)]
        first = ma_at == 0
        mine = jnp.where(first, pool_in[0], pool_pre[0])
        mine = jnp.concatenate([mine, jnp.full((16, DR), pool_len[0], jnp.bfloat16)], axis=0)

        key_slices, value_slices = [], []
        piece = quarter_of(key_weight)
        for step in range(1, pa_count):
            piece = ring_step(piece)
            key_slices.append(plane_gather(piece, 1 + step % 2))
        piece = ring_step(after(quarter_of(value_weight), piece))
        mine = after(mine, piece)
        mine = [mine] + [
            lax.ppermute(mine, "pa", [((i + s) % pa_count, i) for i in range(pa_count)])
            for s in range(1, pa_count)
        ]
        plane_ready = after(piece, key_slices[-1][1], key_slices[-1][2])
        value_slices.append(plane_gather(plane_ready, 2))
        piece = after(piece, *mine)
        for step in range(2, pa_count):
            piece = ring_step(piece)
            value_slices.append(plane_gather(piece, 2 - step % 2))

        keys = running(None, [(own_rows, [key_weight]), (other_rows[0], key_slices[0])])
        for rows_in, slices in list(zip(other_rows, key_slices))[1:-1]:
            keys = running(keys, [(rows_in, slices)])
        last_keys = (keys, [(other_rows[-1], key_slices[-1])])
    else:
        whole = lax.all_gather(key_weight, "pa", axis=0, tiled=True)
        last_keys = (None, [(token_rows, [whole])])
    weights, stats = scores_of(*last_keys, query_blocks, valid, p_here)
    own_stats = stats
    if grouped:
        mine = jnp.stack(mine)
        mine = after(mine, own_stats)
        other = lax.ppermute(mine, "ma", ma_flip)
        inputs = jnp.where(first, mine, other)[:, :tokens]
        pre = jnp.where(first, other, mine)[:, :tokens]
        lengths = mine[:, tokens, 0].astype(jnp.float32)
    else:
        inputs, pre, lengths = pool_in, pool_pre, pool_len.astype(jnp.float32)
    count = inputs.shape[0]

    if grouped:
        stats = jnp.stack(
            [stats]
            + [
                lax.ppermute(stats, "pa", [((i + s) % pa_count, i) for i in range(pa_count)])
                for s in range(1, pa_count)
            ]
        )
    else:
        stats = jnp.roll(lax.all_gather(stats, "pa", axis=0, tiled=False), -pa_at, axis=0)

    query_r = retr_query[0]
    pre_f = pre.astype(jnp.float32)
    centre = pre_f - jnp.mean(pre_f, axis=-1, keepdims=True)
    spread = jnp.mean(centre * centre, axis=-1, keepdims=True)
    inverse = 1.0 / jnp.sqrt(spread + 1e-05)
    normed = centre * inverse
    live = (positions[None, :] < lengths[:, None]).astype(jnp.float32)[..., None]
    embed = jnp.sum(normed * norm_gain * live, axis=1) / lengths[:, None]
    sims = jnp.sum(embed * query_r, axis=-1)
    dnorm = query_r * live * norm_gain / lengths[:, None, None]
    dpre = (
        dnorm
        - jnp.mean(dnorm, axis=-1, keepdims=True)
        - normed * jnp.mean(dnorm * normed, axis=-1, keepdims=True)
    ) * inverse
    dpre_b = dpre.astype(jnp.bfloat16)
    upper = jnp.einsum("krd,df->krf", inputs, up_weight, preferred_element_type=jnp.float32) + up_bias
    act_b = gelu_exact(upper).astype(jnp.bfloat16)
    dact = jnp.einsum("krd,df->krf", dpre_b, down_weight, preferred_element_type=jnp.float32)
    dup_b = (dact * gelu_slope(upper)).astype(jnp.bfloat16)
    dup_own = dup_b[0]
    dpre_own = dpre[0]
    partial_back = jnp.einsum("rf,df->rd", dup_own, up_weight, preferred_element_type=jnp.float32)
    grad_in = dpre_own + partial_back + lax.ppermute(partial_back, "ma", ma_flip)

    def own_columns(values):
        if not grouped:
            return values
        parts = values.reshape(count, tokens, pb_count, pa_count, rows)
        return lax.dynamic_index_in_dim(parts, pa_at, 3, keepdims=False).reshape(count, tokens, pb_count * rows)

    grad_up = jnp.einsum("krd,krf->kdf", own_columns(inputs), dup_b, preferred_element_type=jnp.float32)
    grad_down = jnp.einsum("krd,krf->kdf", own_columns(dpre_b), act_b, preferred_element_type=jnp.float32)

    best = jnp.max(stats[:, 0], axis=0)
    factor = jnp.exp(stats[:, 0] - best[None])
    sums_all = stats[:, 1:] * factor[:, None]
    totals = jnp.sum(sums_all, axis=(0, 1))
    mass = jnp.sum(sums_all / totals, axis=-1) / (ANS * HEADS)
    mass = mass + lax.ppermute(mass, "ma", ma_flip)
    mass = jnp.roll(mass, pa_at, axis=0).reshape(pa_count * p_here)
    if grouped:
        sims = jnp.roll(sims, pa_at)
    else:
        sims = lax.all_gather(sims, "pa", axis=0, tiled=True)
    where_at = placement_perm[0][passage_ids[0]]
    p_ret = jax.nn.softmax(sims[where_at])
    coef = loss_scale * (p_ret - mass)
    held = (jnp.arange(count, dtype=jnp.int32) + pa_at) % pa_count
    scalars = jnp.sum(jnp.where(where_at[None, :] == held[:, None], coef[None, :], 0.0), axis=1)

    pool_grad = (grad_in * scalars[0]).astype(jnp.bfloat16)[None]

    def scatter_sum(grads, bits):
        total = grads[0] * scalars[0]
        for k in range(1, count):
            total = total + grads[k] * scalars[k]
        if not grouped:
            total = jnp.transpose(total.reshape(pb_count, pa_count, rows, ff_here), (1, 0, 2, 3))
            total = lax.psum_scatter(total, "pa", scatter_dimension=0, tiled=False)
        parts = total.reshape(pb_count, rows, ff_here)
        for bit in bits:
            split = parts.reshape((-1, 2, bit if parts.shape[0] == pb_count else 1) + parts.shape[1:])
            side = (pb_at // bit) % 2
            keep = lax.dynamic_index_in_dim(split, side, 1, keepdims=False)
            give = lax.dynamic_index_in_dim(split, 1 - side, 1, keepdims=False)
            got = flip(give.astype(jnp.bfloat16), bit)
            parts = (keep + got.astype(jnp.float32)).reshape((-1,) + parts.shape[1:])
        return parts[0]

    up_grad = scatter_sum(grad_up, (1, 2))
    down_grad = scatter_sum(grad_down, (2, 1))

    if grouped:
        values_own = after(own_rows, grad_up, grad_down)
        values = running(None, [(values_own, [value_weight]), (other_rows[0], value_slices[0])])
        for rows_in, slices in list(zip(other_rows, value_slices))[1:-1]:
            values = running(values, [(rows_in, slices)])
        last_values = (values, [(other_rows[-1], value_slices[-1])])
    else:
        whole = lax.all_gather(value_weight, "pa", axis=0, tiled=True)
        last_values = (None, [(token_rows, [whole])])
    summed = summed_of(*last_values, weights, (factor[0] / totals)[None])
    if grouped:
        step = 1
        while step < pa_count:
            summed = summed + lax.ppermute(summed, "pa", [(i, i ^ step) for i in range(pa_count)])
            step *= 2
    else:
        summed = lax.psum(summed, "pa")
    attn_out = summed.astype(jnp.bfloat16).reshape(q_here, ANS, cols_here)
    return (attn_out, pool_grad, up_grad, down_grad)


def solution(mesh):
    return jax.shard_map(
        local,
        mesh=mesh,
        in_specs=(
            P("pb", "pa", None, None),
            P("pa", "ma"),
            P("pa", "ma"),
            P("pb", None, "ma"),
            P("pb", "pa"),
            P("pb", None),
            P("pb", None),
            P("pb", None),
            P(("pb", "pa"), None, None),
            P(("pb", "pa"), None, None),
            P(("pb", "pa")),
            P(None, "ma"),
            P("ma"),
            P(None, "ma"),
            P(),
        ),
        out_specs=(
            P("pb", None, "ma"),
            P(("pb", "pa"), None, None),
            P(("pb", "pa"), "ma"),
            P(("pb", "pa"), "ma"),
        ),
        check_vma=False,
    )
```

```python
import jax
import jax.numpy as jnp
from jax import lax
from jax.experimental import pallas as pl
from jax.experimental.pallas import tpu as pltpu
from jax.sharding import PartitionSpec as P

HEADS = 32
HDIM = 64
ANS = 32
DR = 768


RING_MOST = 4


loss_scale = 16384.0
highest = lax.Precision.HIGHEST


def ring_order(count):
    return list(range(0, count, 2)) + [i for i in range(count - 1, 0, -1) if i % 2]


def ring_next(count):
    order = ring_order(count)
    return [(order[i], order[(i + 1) % count]) for i in range(count)]


def flip(values, bit):
    count = lax.axis_size("pb")
    return lax.ppermute(values, "pb", [(i, i ^ bit) for i in range(count)])


def after(value, *others):
    return lax.optimization_barrier((value,) + others)[0]


def plane_slots(count):
    if count == 6:
        x = ["a0", "a1", "b0", "a2", "b2", "a3", "a4", "a5", "b4"]
        y = ["a0", "a1", "a2", "b1", "a3", "a4", "a5", "b3", "b5"]
    else:
        x, y = [], []
        for r in range(count):
            x.append(f"a{r}")
            y.append(f"a{r}")
            (x, y)[r % 2].append(f"b{r}")
    return [[(slot[0], int(slot[1:])) for slot in link] for link in (x, y)]


class PlaneGathers:
    def __init__(self, ring):
        self.ring = ring
        self.left = plane_slots(len(ring))
        self.got = {}
        self.turns = []

    def turn(self, *others):
        now = []
        for link in (0, 1):
            if not self.left[link]:
                continue
            kind, r = self.left[link][0]
            if kind == "b" and (1 - link, "a", r) not in self.got:
                continue
            self.left[link].pop(0)
            data = self.ring[r] if kind == "a" else self.got[(1 - link, "a", r)]
            before = (self.turns[-2] if len(self.turns) > 1 else []) + list(others)
            if before:
                data = after(data, *before)
            now.append((link, kind, r, flip(data, 1 + link)))
        for link, kind, r, value in now:
            self.got[(link, kind, r)] = value
        self.turns.append([value for _, _, _, value in now])
        return bool(self.left[0] or self.left[1])

    def slice(self, r):
        return [self.ring[r], self.got[(0, "a", r)], self.got[(1, "a", r)], self.got[(r % 2, "b", r)]]


LENGTH_ROWS = 16
COLUMNS = 256


def accumulate(refs, has_total, count):
    total = refs[0][...] if has_total else None
    at = 1 if has_total else 0
    for _ in range(count):
        term = jnp.dot(refs[at][...], refs[at + 1][...], preferred_element_type=jnp.float32)
        total = term if total is None else total + term
        at += 2
    return total, refs[at:]


def two_terms(values):
    high = values.astype(jnp.bfloat16)
    return high, (values - high.astype(jnp.float32)).astype(jnp.bfloat16)


def projection(total, rows, pairs, finish, extra, extra_specs, out_shape, out_specs):
    arrays = [] if total is None else [total]
    specs = [] if total is None else [pl.BlockSpec((total.shape[0], COLUMNS), lambda i, at: (0, i))]
    flops = 0
    for n, (_, part) in enumerate(pairs):
        arrays += [rows, part]
        specs += [
            pl.BlockSpec((rows.shape[0], part.shape[0]), lambda i, at, n=n: (0, at[n])),
            pl.BlockSpec((part.shape[0], COLUMNS), lambda i, at: (0, i)),
        ]
        flops += 2 * rows.shape[0] * part.shape[0] * part.shape[1]
    places = jnp.stack([jnp.asarray(place, jnp.int32) for place, _ in pairs])

    def kernel(places_ref, *refs):
        value, rest = accumulate(refs, total is not None, len(pairs))
        finish(value, *rest)

    return pl.pallas_call(
        kernel,
        grid_spec=pltpu.PrefetchScalarGridSpec(
            num_scalar_prefetch=1,
            grid=(pairs[0][1].shape[1] // COLUMNS,),
            in_specs=specs + list(extra_specs),
            out_specs=out_specs,
        ),
        out_shape=out_shape,
        compiler_params=pltpu.CompilerParams(vmem_limit_bytes=32 << 20),
        cost_estimate=pl.CostEstimate(flops=flops, bytes_accessed=8 << 20, transcendentals=0),
    )(places, *arrays, *extra)


def store(value, out_ref):
    out_ref[...] = value


def running(total, rows, pairs):
    tokens, columns = rows.shape[0], pairs[0][1].shape[1]
    return projection(
        total,
        rows,
        pairs,
        store,
        (),
        (),
        jax.ShapeDtypeStruct((tokens, columns), jnp.float32),
        pl.BlockSpec((tokens, COLUMNS), lambda i, at: (0, i)),
    )


def scores_of(total, rows, pairs, query_blocks, valid, p_here):
    tokens = rows.shape[0]
    queries = query_blocks.shape[1]
    blocks = pairs[0][1].shape[1] // COLUMNS
    each = tokens // p_here

    def finish(keys, query_ref, valid_ref, weight_ref, stat_ref):
        high, low = two_terms(keys)
        query = query_ref[...]
        scores = jnp.dot(high, query, preferred_element_type=jnp.float32)
        scores = scores + jnp.dot(low, query, preferred_element_type=jnp.float32)
        alive = valid_ref[...] > 0.0
        scores = jnp.where(alive, scores, -1e30)
        top = jnp.max(scores, axis=0, keepdims=True)
        weights = jnp.where(alive, jnp.exp(scores - top), 0.0)
        weight_ref[...] = weights
        lines = [top] + [
            jnp.sum(weights[p * each : (p + 1) * each], axis=0, keepdims=True) for p in range(p_here)
        ]
        for i, row in enumerate(lines):
            stat_ref[i : i + 1, :] = row

    wide = queries // blocks
    return projection(
        total,
        rows,
        pairs,
        finish,
        (query_blocks, valid),
        (
            pl.BlockSpec((COLUMNS, wide), lambda i, at: (0, i)),
            pl.BlockSpec((tokens, wide), lambda i, at: (0, 0)),
        ),
        (
            jax.ShapeDtypeStruct((tokens, queries), jnp.float32),
            jax.ShapeDtypeStruct((1 + p_here, queries), jnp.float32),
        ),
        (
            pl.BlockSpec((tokens, wide), lambda i, at: (0, i)),
            pl.BlockSpec((1 + p_here, wide), lambda i, at: (0, i)),
        ),
    )


def summed_of(total, rows, pairs, weights, ratio):
    tokens, queries = weights.shape
    columns = pairs[0][1].shape[1]
    blocks = columns // COLUMNS
    wide = queries // blocks

    def finish(values, weight_ref, ratio_ref, out_ref):
        high, low = two_terms(values)
        w_high, w_low = two_terms(weight_ref[...] * ratio_ref[...])
        over = (((0,), (0,)), ((), ()))
        full = lax.dot_general(w_high, high, over, preferred_element_type=jnp.float32)
        full = full + lax.dot_general(w_high, low, over, preferred_element_type=jnp.float32)
        full = full + lax.dot_general(w_low, high, over, preferred_element_type=jnp.float32)
        head = lax.broadcasted_iota(jnp.int32, (ANS, COLUMNS), 1) // HDIM
        out = jnp.zeros((ANS, COLUMNS), jnp.float32)
        for h in range(COLUMNS // HDIM):
            out = jnp.where(head == h, full[h * ANS : (h + 1) * ANS], out)
        out_ref[...] = out

    return projection(
        total,
        rows,
        pairs,
        finish,
        (weights, ratio),
        (
            pl.BlockSpec((tokens, wide), lambda i, at: (0, i)),
            pl.BlockSpec((1, wide), lambda i, at: (0, i)),
        ),
        jax.ShapeDtypeStruct((ANS, columns), jnp.float32),
        pl.BlockSpec((ANS, COLUMNS), lambda i, at: (0, i)),
    )


def backward_kernel(
    place_ref, mine_ref, other_ref, up_ref, bias_ref, down_ref, gain_ref, query_ref, chosen_ref,
    grad_up_ref, grad_down_ref, sim_ref, dpre_ref, dup_ref,
):
    tokens = mine_ref.shape[1] - LENGTH_ROWS
    mine = mine_ref[0].astype(jnp.float32)
    other = other_ref[0].astype(jnp.float32)
    swap = place_ref[0] != 0
    inputs = jnp.where(swap, other, mine)[:tokens].astype(jnp.bfloat16)
    pre = jnp.where(swap, mine, other)[:tokens]
    length = mine[tokens : tokens + 1, 0:1]
    gain, query = gain_ref[...], query_ref[...]
    centre = pre - jnp.mean(pre, axis=-1, keepdims=True)
    spread = jnp.mean(centre * centre, axis=-1, keepdims=True)
    inverse = 1.0 / jnp.sqrt(spread + 1e-05)
    normed = centre * inverse
    position = lax.broadcasted_iota(jnp.int32, (tokens, 1), 0).astype(jnp.float32)
    live = (position < length).astype(jnp.float32)
    embed = jnp.sum(normed * gain * live, axis=0, keepdims=True) / length
    sim = jnp.sum(embed * query, axis=-1, keepdims=True)
    sim_ref[0] = jnp.broadcast_to(sim, sim_ref.shape[1:])
    dnorm = query * live * gain / length
    dpre = (
        dnorm
        - jnp.mean(dnorm, axis=-1, keepdims=True)
        - normed * jnp.mean(dnorm * normed, axis=-1, keepdims=True)
    ) * inverse
    dpre_b = dpre.astype(jnp.bfloat16)
    chosen = chosen_ref[...]
    inputs_part = jnp.dot(inputs, chosen, preferred_element_type=jnp.float32).astype(jnp.bfloat16)
    dpre_part = jnp.dot(dpre_b, chosen, preferred_element_type=jnp.float32).astype(jnp.bfloat16)
    over = (((0,), (0,)), ((), ()))
    wide = 512
    for start in range(0, up_ref.shape[1], wide):
        cols = slice(start, start + wide)
        upper = jnp.dot(inputs, up_ref[:, cols], preferred_element_type=jnp.float32) + bias_ref[:, cols]
        dact = jnp.dot(dpre_b, down_ref[:, cols], preferred_element_type=jnp.float32)
        below = 0.5 * (1.0 + lax.erf(upper * 0.7071067811865476))
        act_b = (upper * below).astype(jnp.bfloat16)
        slope = below + upper * jnp.exp(-0.5 * upper * upper) * 0.3989422804014327
        dup_b = (dact * slope).astype(jnp.bfloat16)
        grad_up_ref[0, :, cols] = lax.dot_general(inputs_part, dup_b, over, preferred_element_type=jnp.float32)
        grad_down_ref[0, :, cols] = lax.dot_general(dpre_part, act_b, over, preferred_element_type=jnp.float32)

        @pl.when(pl.program_id(0) == 0)
        def _():
            dup_ref[:, cols] = dup_b

    @pl.when(pl.program_id(0) == 0)
    def _():
        dpre_ref[...] = dpre


def backward(place, mine, other, up_weight, up_bias, down_weight, gain, query, chosen):
    count, padded, width = mine.shape
    tokens = padded - LENGTH_ROWS
    hidden, part = up_weight.shape[1], chosen.shape[1]
    whole = lambda array: pl.BlockSpec(array.shape, lambda k, at: (0, 0))
    one = lambda *shape: pl.BlockSpec((1,) + shape, lambda k, at: (k, 0, 0))
    fixed = lambda *shape: pl.BlockSpec(shape, lambda k, at: (0, 0))
    flops = 4 * count * tokens * hidden * (width + part)
    return pl.pallas_call(
        backward_kernel,
        grid_spec=pltpu.PrefetchScalarGridSpec(
            num_scalar_prefetch=1,
            grid=(count,),
            in_specs=[one(padded, width), one(padded, width)]
            + [whole(a) for a in (up_weight, up_bias, down_weight, gain, query, chosen)],
            out_specs=[one(part, hidden), one(part, hidden), one(1, 128), fixed(tokens, width), fixed(tokens, hidden)],
        ),
        out_shape=[
            jax.ShapeDtypeStruct((count, part, hidden), jnp.float32),
            jax.ShapeDtypeStruct((count, part, hidden), jnp.float32),
            jax.ShapeDtypeStruct((count, 1, 128), jnp.float32),
            jax.ShapeDtypeStruct((tokens, width), jnp.float32),
            jax.ShapeDtypeStruct((tokens, hidden), jnp.bfloat16),
        ],
        compiler_params=pltpu.CompilerParams(vmem_limit_bytes=48 << 20),
        cost_estimate=pl.CostEstimate(flops=flops, bytes_accessed=24 << 20, transcendentals=2 * count * tokens * hidden),
    )(place, mine, other, up_weight, up_bias, down_weight, gain, query, chosen)


def quarter_of(weight):
    quarter = weight.shape[0] // lax.axis_size("pb")
    return lax.dynamic_slice_in_dim(weight, lax.axis_index("pb") * quarter, quarter, 0)


def ring_step(piece):
    return lax.ppermute(piece, "pa", ring_next(lax.axis_size("pa")))


def local(
    encoded,
    key_weight,
    value_weight,
    queries,
    key_len,
    retr_query,
    passage_ids,
    placement_perm,
    pool_in,
    pool_pre,
    pool_len,
    up_weight,
    up_bias,
    down_weight,
    norm_gain,
):
    q_here, p_here, tokens, width = encoded.shape
    pb_count = lax.axis_size("pb")
    pa_count = lax.axis_size("pa")
    ma_count = lax.axis_size("ma")
    pb_at = lax.axis_index("pb")
    pa_at = lax.axis_index("pa")
    ma_at = lax.axis_index("ma")
    heads_here = HEADS // ma_count
    cols_here = key_weight.shape[1]
    depth = key_weight.shape[0]
    token_rows = encoded.reshape(p_here * tokens, width)

    order = jnp.array(ring_order(pa_count), jnp.int32)
    place = jnp.argmax(order == pa_at).astype(jnp.int32)

    def owner_of(step):
        return order[(place - step + pa_count) % pa_count]

    def placed(step, parts):
        return [(owner_of(step) * pb_count + (pb_at ^ q), part) for q, part in enumerate(parts)]

    positions = jnp.arange(tokens, dtype=jnp.int32)
    grouped = pa_count <= RING_MOST
    rows = DR // (pb_count * pa_count)
    ff_here = up_weight.shape[1]
    ma_flip = [(i, ma_count - 1 - i) for i in range(ma_count)]
    blocks = cols_here // COLUMNS
    in_block = COLUMNS // HDIM
    pairs = ANS * heads_here
    same = jnp.eye(in_block, dtype=jnp.bfloat16)
    query_blocks = jnp.einsum(
        "abgj,gh->gjbha", queries[0].reshape(ANS, blocks, in_block, HDIM), same
    ).reshape(COLUMNS, pairs)
    valid = (positions[None, :] < key_len[0][:, None]).astype(jnp.float32).reshape(-1, 1)
    valid = jnp.broadcast_to(valid, (p_here * tokens, pairs // blocks))
    if grouped:
        first = ma_at == 0
        mine = jnp.where(first, pool_in[0], pool_pre[0])
        mine = jnp.concatenate([mine, jnp.full((LENGTH_ROWS, DR), pool_len[0], jnp.bfloat16)], axis=0)

        ring = []
        for weight in (key_weight, value_weight):
            piece = quarter_of(weight)
            if ring:
                piece = after(piece, ring[-1])
            for _ in range(pa_count - 1):
                if len(ring) == 2 * pa_count - 3:
                    mine = after(mine, piece)
                    mine = [mine] + [
                        lax.ppermute(mine, "pa", [((i + s) % pa_count, i) for i in range(pa_count)])
                        for s in range(1, pa_count)
                    ]
                piece = ring_step(piece)
                ring.append(piece)
        plane = PlaneGathers(ring)
        while (pa_count % 2, "b", pa_count - 2) not in plane.got:
            plane.turn()
        key_slices = [plane.slice(r) for r in range(pa_count - 1)]
    else:
        whole = lax.all_gather(key_weight, "pa", axis=0, tiled=True)
        weights, stats = scores_of(None, token_rows, [(0, whole)], query_blocks, valid, p_here)
    if grouped:
        keys = running(None, token_rows, [(pa_at, key_weight)] + placed(1, key_slices[0]))
        keys = running(keys, token_rows, placed(2, key_slices[1]))
        rest = [pair for step in range(3, pa_count) for pair in placed(step, key_slices[step - 1])]
        weights, stats = scores_of(keys, token_rows, rest, query_blocks, valid, p_here)
    if grouped:
        mine = after(jnp.stack(mine), stats)
        other = lax.ppermute(mine, "ma", ma_flip)
        inputs_in = ma_at
    else:
        lengths = jnp.full((1, LENGTH_ROWS, DR), pool_len[0], jnp.bfloat16)
        mine = jnp.concatenate([pool_in, lengths], axis=1)
        other = jnp.concatenate([pool_pre, lengths], axis=1)
        inputs_in = 0
    count = mine.shape[0]

    block = jnp.arange(DR, dtype=jnp.int32)
    if grouped:
        kept = jnp.arange(pb_count * rows, dtype=jnp.int32)
        kept = (kept // rows * pa_count + pa_at) * rows + kept % rows
    else:
        kept = block
    chosen = (block[:, None] == kept[None, :]).astype(jnp.bfloat16)
    grad_up, grad_down, sims, dpre, dup_b = backward(
        jnp.asarray(inputs_in, jnp.int32).reshape(1),
        mine,
        other,
        up_weight,
        up_bias[None],
        down_weight,
        norm_gain[None],
        retr_query,
        chosen,
    )
    sims = sims[:, 0, 0]
    if grouped:
        plane.turn()
        plane.turn()
        plane.turn()
        early = set(plane.got)
        while plane.turn(grad_up, grad_down):
            pass
    partial_back = jnp.einsum("rf,df->rd", dup_b, up_weight, preferred_element_type=jnp.float32)
    grad_in = dpre + partial_back + lax.ppermute(partial_back, "ma", ma_flip)

    if grouped:
        stats = jnp.stack(
            [stats]
            + [
                lax.ppermute(stats, "pa", [((i + s) % pa_count, i) for i in range(pa_count)])
                for s in range(1, pa_count)
            ]
        )
    else:
        stats = jnp.roll(lax.all_gather(stats, "pa", axis=0, tiled=False), -pa_at, axis=0)
    best = jnp.max(stats[:, 0], axis=0)
    factor = jnp.exp(stats[:, 0] - best[None])
    sums_all = stats[:, 1:] * factor[:, None]
    totals = jnp.sum(sums_all, axis=(0, 1))
    mass = jnp.sum(sums_all / totals, axis=-1) / (ANS * HEADS)
    mass = mass + lax.ppermute(mass, "ma", ma_flip)
    mass = jnp.roll(mass, pa_at, axis=0).reshape(pa_count * p_here)
    if grouped:
        sims = jnp.roll(sims, pa_at)
    else:
        sims = lax.all_gather(sims, "pa", axis=0, tiled=True)
    where_at = placement_perm[0][passage_ids[0]]
    p_ret = jax.nn.softmax(sims[where_at])
    coef = loss_scale * (p_ret - mass)
    held = (jnp.arange(count, dtype=jnp.int32) + pa_at) % pa_count
    scalars = jnp.sum(jnp.where(where_at[None, :] == held[:, None], coef[None, :], 0.0), axis=1)

    pool_grad = (grad_in * scalars[0]).astype(jnp.bfloat16)[None]

    def scatter_sum(grads, bits):
        total = grads[0] * scalars[0]
        for k in range(1, count):
            total = total + grads[k] * scalars[k]
        if not grouped:
            total = jnp.transpose(total.reshape(pb_count, pa_count, rows, ff_here), (1, 0, 2, 3))
            total = lax.psum_scatter(total, "pa", scatter_dimension=0, tiled=False)
        parts = total.reshape(pb_count, rows, ff_here)
        for bit in bits:
            split = parts.reshape((-1, 2, bit if parts.shape[0] == pb_count else 1) + parts.shape[1:])
            side = (pb_at // bit) % 2
            keep = lax.dynamic_index_in_dim(split, side, 1, keepdims=False)
            give = lax.dynamic_index_in_dim(split, 1 - side, 1, keepdims=False)
            got = flip(give.astype(jnp.bfloat16), bit)
            parts = (keep + got.astype(jnp.float32)).reshape((-1,) + parts.shape[1:])
        return parts[0]

    up_grad = scatter_sum(grad_up, (1, 2))
    down_grad = scatter_sum(grad_down, (2, 1))

    if grouped:
        ready, late = [(pa_at, value_weight)], []
        for r in range(pa_count - 1, 2 * (pa_count - 1)):
            step = r - pa_count + 2
            keys_of = [None, (0, "a", r), (1, "a", r), (r % 2, "b", r)]
            for key, pair in zip(keys_of, placed(step, plane.slice(r))):
                (ready if key is None or key in early else late).append(pair)
        values = running(None, after(token_rows, grad_up, grad_down), ready)
        last_values = (values, token_rows, late)
    else:
        whole = lax.all_gather(value_weight, "pa", axis=0, tiled=True)
        last_values = (None, token_rows, [(0, whole)])
    summed = summed_of(*last_values, weights, (factor[0] / totals)[None])
    if grouped:
        step = 1
        while step < pa_count:
            summed = summed + lax.ppermute(summed, "pa", [(i, i ^ step) for i in range(pa_count)])
            step *= 2
    else:
        summed = lax.psum(summed, "pa")
    attn_out = summed.astype(jnp.bfloat16).reshape(q_here, ANS, cols_here)
    return (attn_out, pool_grad, up_grad, down_grad)


def solution(mesh):
    return jax.shard_map(
        local,
        mesh=mesh,
        in_specs=(
            P("pb", "pa", None, None),
            P("pa", "ma"),
            P("pa", "ma"),
            P("pb", None, "ma"),
            P("pb", "pa"),
            P("pb", None),
            P("pb", None),
            P("pb", None),
            P(("pb", "pa"), None, None),
            P(("pb", "pa"), None, None),
            P(("pb", "pa")),
            P(None, "ma"),
            P("ma"),
            P(None, "ma"),
            P(),
        ),
        out_specs=(
            P("pb", None, "ma"),
            P(("pb", "pa"), None, None),
            P(("pb", "pa"), "ma"),
            P(("pb", "pa"), "ma"),
        ),
        check_vma=False,
    )
```

```python
import jax
import jax.numpy as jnp
from jax import lax
from jax.experimental import pallas as pl
from jax.experimental.pallas import tpu as pltpu
from jax.sharding import PartitionSpec as P

HEADS = 32
HDIM = 64
ANS = 32
DR = 768


RING_MOST = 4


loss_scale = 16384.0
highest = lax.Precision.HIGHEST


def ring_order(count):
    return list(range(0, count, 2)) + [i for i in range(count - 1, 0, -1) if i % 2]


def ring_next(count):
    order = ring_order(count)
    return [(order[i], order[(i + 1) % count]) for i in range(count)]


def flip(values, bit):
    count = lax.axis_size("pb")
    return lax.ppermute(values, "pb", [(i, i ^ bit) for i in range(count)])


def after(value, *others):
    return lax.optimization_barrier((value,) + others)[0]


def plane_slots(count):
    if count == 6:
        x = ["a0", "a1", "b0", "a2", "b2", "a3", "a4", "a5", "b4"]
        y = ["a0", "a1", "a2", "b1", "a3", "a4", "a5", "b3", "b5"]
    else:
        x, y = [], []
        for r in range(count):
            x.append(f"a{r}")
            y.append(f"a{r}")
            (x, y)[r % 2].append(f"b{r}")
    return [[(slot[0], int(slot[1:])) for slot in link] for link in (x, y)]


class PlaneGathers:
    def __init__(self, ring):
        self.ring = ring
        self.left = plane_slots(len(ring))
        self.got = {}
        self.turns = []

    def turn(self, *others):
        now = []
        for link in (0, 1):
            if not self.left[link]:
                continue
            kind, r = self.left[link][0]
            if kind == "b" and (1 - link, "a", r) not in self.got:
                continue
            self.left[link].pop(0)
            data = self.ring[r] if kind == "a" else self.got[(1 - link, "a", r)]
            before = (self.turns[-2] if len(self.turns) > 1 else []) + list(others)
            if before:
                data = after(data, *before)
            now.append((link, kind, r, flip(data, 1 + link)))
        for link, kind, r, value in now:
            self.got[(link, kind, r)] = value
        self.turns.append([value for _, _, _, value in now])
        return bool(self.left[0] or self.left[1])

    def slice(self, r):
        return [self.ring[r], self.got[(0, "a", r)], self.got[(1, "a", r)], self.got[(r % 2, "b", r)]]


LENGTH_ROWS = 16
COLUMNS = 256


def accumulate(refs, has_total, count):
    total = refs[0][...] if has_total else None
    at = 1 if has_total else 0
    for _ in range(count):
        term = jnp.dot(refs[at][...], refs[at + 1][...], preferred_element_type=jnp.float32)
        total = term if total is None else total + term
        at += 2
    return total, refs[at:]


def two_terms(values):
    high = values.astype(jnp.bfloat16)
    return high, (values - high.astype(jnp.float32)).astype(jnp.bfloat16)


def projection(total, rows, pairs, finish, extra, extra_specs, out_shape, out_specs):
    arrays = [] if total is None else [total]
    specs = [] if total is None else [pl.BlockSpec((total.shape[0], COLUMNS), lambda i, at: (0, i))]
    flops = 0
    for n, (_, part) in enumerate(pairs):
        arrays += [rows, part]
        specs += [
            pl.BlockSpec((rows.shape[0], part.shape[0]), lambda i, at, n=n: (0, at[n])),
            pl.BlockSpec((part.shape[0], COLUMNS), lambda i, at: (0, i)),
        ]
        flops += 2 * rows.shape[0] * part.shape[0] * part.shape[1]
    places = jnp.stack([jnp.asarray(place, jnp.int32) for place, _ in pairs])

    def kernel(places_ref, *refs):
        value, rest = accumulate(refs, total is not None, len(pairs))
        finish(value, *rest)

    return pl.pallas_call(
        kernel,
        grid_spec=pltpu.PrefetchScalarGridSpec(
            num_scalar_prefetch=1,
            grid=(pairs[0][1].shape[1] // COLUMNS,),
            in_specs=specs + list(extra_specs),
            out_specs=out_specs,
        ),
        out_shape=out_shape,
        compiler_params=pltpu.CompilerParams(vmem_limit_bytes=32 << 20),
        cost_estimate=pl.CostEstimate(flops=flops, bytes_accessed=8 << 20, transcendentals=0),
    )(places, *arrays, *extra)


def store(value, out_ref):
    out_ref[...] = value


def running(total, rows, pairs):
    tokens, columns = rows.shape[0], pairs[0][1].shape[1]
    return projection(
        total,
        rows,
        pairs,
        store,
        (),
        (),
        jax.ShapeDtypeStruct((tokens, columns), jnp.float32),
        pl.BlockSpec((tokens, COLUMNS), lambda i, at: (0, i)),
    )


def scores_of(total, rows, pairs, query_blocks, valid, p_here):
    tokens = rows.shape[0]
    queries = query_blocks.shape[1]
    blocks = pairs[0][1].shape[1] // COLUMNS
    each = tokens // p_here

    def finish(keys, query_ref, valid_ref, weight_ref, stat_ref):
        high, low = two_terms(keys)
        query = query_ref[...]
        scores = jnp.dot(high, query, preferred_element_type=jnp.float32)
        scores = scores + jnp.dot(low, query, preferred_element_type=jnp.float32)
        alive = valid_ref[...] > 0.0
        scores = jnp.where(alive, scores, -1e30)
        top = jnp.max(scores, axis=0, keepdims=True)
        weights = jnp.where(alive, jnp.exp(scores - top), 0.0)
        weight_ref[...] = weights
        lines = [top] + [
            jnp.sum(weights[p * each : (p + 1) * each], axis=0, keepdims=True) for p in range(p_here)
        ]
        for i, row in enumerate(lines):
            stat_ref[i : i + 1, :] = row

    wide = queries // blocks
    return projection(
        total,
        rows,
        pairs,
        finish,
        (query_blocks, valid),
        (
            pl.BlockSpec((COLUMNS, wide), lambda i, at: (0, i)),
            pl.BlockSpec((tokens, wide), lambda i, at: (0, 0)),
        ),
        (
            jax.ShapeDtypeStruct((tokens, queries), jnp.float32),
            jax.ShapeDtypeStruct((1 + p_here, queries), jnp.float32),
        ),
        (
            pl.BlockSpec((tokens, wide), lambda i, at: (0, i)),
            pl.BlockSpec((1 + p_here, wide), lambda i, at: (0, i)),
        ),
    )


def summed_of(total, rows, pairs, weights, ratio):
    tokens, queries = weights.shape
    columns = pairs[0][1].shape[1]
    blocks = columns // COLUMNS
    wide = queries // blocks

    def finish(values, weight_ref, ratio_ref, out_ref):
        high, low = two_terms(values)
        w_high, w_low = two_terms(weight_ref[...] * ratio_ref[...])
        over = (((0,), (0,)), ((), ()))
        full = lax.dot_general(w_high, high, over, preferred_element_type=jnp.float32)
        full = full + lax.dot_general(w_high, low, over, preferred_element_type=jnp.float32)
        full = full + lax.dot_general(w_low, high, over, preferred_element_type=jnp.float32)
        head = lax.broadcasted_iota(jnp.int32, (ANS, COLUMNS), 1) // HDIM
        out = jnp.zeros((ANS, COLUMNS), jnp.float32)
        for h in range(COLUMNS // HDIM):
            out = jnp.where(head == h, full[h * ANS : (h + 1) * ANS], out)
        out_ref[...] = out

    return projection(
        total,
        rows,
        pairs,
        finish,
        (weights, ratio),
        (
            pl.BlockSpec((tokens, wide), lambda i, at: (0, i)),
            pl.BlockSpec((1, wide), lambda i, at: (0, i)),
        ),
        jax.ShapeDtypeStruct((ANS, columns), jnp.float32),
        pl.BlockSpec((ANS, COLUMNS), lambda i, at: (0, i)),
    )


def backward_kernel(
    place_ref, mine_ref, other_ref, up_ref, bias_ref, down_ref, gain_ref, query_ref, chosen_ref,
    grad_up_ref, grad_down_ref, sim_ref, dpre_ref, dup_ref,
):
    tokens = mine_ref.shape[1] - LENGTH_ROWS
    mine = mine_ref[0].astype(jnp.float32)
    other = other_ref[0].astype(jnp.float32)
    swap = place_ref[0] != 0
    inputs = jnp.where(swap, other, mine)[:tokens].astype(jnp.bfloat16)
    pre = jnp.where(swap, mine, other)[:tokens]
    length = mine[tokens : tokens + 1, 0:1]
    gain, query = gain_ref[...], query_ref[...]
    centre = pre - jnp.mean(pre, axis=-1, keepdims=True)
    spread = jnp.mean(centre * centre, axis=-1, keepdims=True)
    inverse = 1.0 / jnp.sqrt(spread + 1e-05)
    normed = centre * inverse
    position = lax.broadcasted_iota(jnp.int32, (tokens, 1), 0).astype(jnp.float32)
    live = (position < length).astype(jnp.float32)
    embed = jnp.sum(normed * gain * live, axis=0, keepdims=True) / length
    sim = jnp.sum(embed * query, axis=-1, keepdims=True)
    sim_ref[0] = jnp.broadcast_to(sim, sim_ref.shape[1:])
    dnorm = query * live * gain / length
    dpre = (
        dnorm
        - jnp.mean(dnorm, axis=-1, keepdims=True)
        - normed * jnp.mean(dnorm * normed, axis=-1, keepdims=True)
    ) * inverse
    dpre_b = dpre.astype(jnp.bfloat16)
    chosen = chosen_ref[...]
    inputs_part = jnp.dot(inputs, chosen, preferred_element_type=jnp.float32).astype(jnp.bfloat16)
    dpre_part = jnp.dot(dpre_b, chosen, preferred_element_type=jnp.float32).astype(jnp.bfloat16)
    over = (((0,), (0,)), ((), ()))
    wide = 512
    for start in range(0, up_ref.shape[1], wide):
        cols = slice(start, start + wide)
        upper = jnp.dot(inputs, up_ref[:, cols], preferred_element_type=jnp.float32) + bias_ref[:, cols]
        dact = jnp.dot(dpre_b, down_ref[:, cols], preferred_element_type=jnp.float32)
        below = 0.5 * (1.0 + lax.erf(upper * 0.7071067811865476))
        act_b = (upper * below).astype(jnp.bfloat16)
        slope = below + upper * jnp.exp(-0.5 * upper * upper) * 0.3989422804014327
        dup_b = (dact * slope).astype(jnp.bfloat16)
        grad_up_ref[0, :, cols] = lax.dot_general(inputs_part, dup_b, over, preferred_element_type=jnp.float32)
        grad_down_ref[0, :, cols] = lax.dot_general(dpre_part, act_b, over, preferred_element_type=jnp.float32)

        @pl.when(pl.program_id(0) == 0)
        def _():
            dup_ref[:, cols] = dup_b

    @pl.when(pl.program_id(0) == 0)
    def _():
        dpre_ref[...] = dpre


def backward(place, mine, other, up_weight, up_bias, down_weight, gain, query, chosen):
    count, padded, width = mine.shape
    tokens = padded - LENGTH_ROWS
    hidden, part = up_weight.shape[1], chosen.shape[1]
    whole = lambda array: pl.BlockSpec(array.shape, lambda k, at: (0, 0))
    one = lambda *shape: pl.BlockSpec((1,) + shape, lambda k, at: (k, 0, 0))
    fixed = lambda *shape: pl.BlockSpec(shape, lambda k, at: (0, 0))
    flops = 4 * count * tokens * hidden * (width + part)
    return pl.pallas_call(
        backward_kernel,
        grid_spec=pltpu.PrefetchScalarGridSpec(
            num_scalar_prefetch=1,
            grid=(count,),
            in_specs=[one(padded, width), one(padded, width)]
            + [whole(a) for a in (up_weight, up_bias, down_weight, gain, query, chosen)],
            out_specs=[one(part, hidden), one(part, hidden), one(1, 128), fixed(tokens, width), fixed(tokens, hidden)],
        ),
        out_shape=[
            jax.ShapeDtypeStruct((count, part, hidden), jnp.float32),
            jax.ShapeDtypeStruct((count, part, hidden), jnp.float32),
            jax.ShapeDtypeStruct((count, 1, 128), jnp.float32),
            jax.ShapeDtypeStruct((tokens, width), jnp.float32),
            jax.ShapeDtypeStruct((tokens, hidden), jnp.bfloat16),
        ],
        compiler_params=pltpu.CompilerParams(vmem_limit_bytes=48 << 20),
        cost_estimate=pl.CostEstimate(flops=flops, bytes_accessed=24 << 20, transcendentals=2 * count * tokens * hidden),
    )(place, mine, other, up_weight, up_bias, down_weight, gain, query, chosen)


def quarter_of(weight):
    quarter = weight.shape[0] // lax.axis_size("pb")
    return lax.dynamic_slice_in_dim(weight, lax.axis_index("pb") * quarter, quarter, 0)


def ring_step(piece):
    return lax.ppermute(piece, "pa", ring_next(lax.axis_size("pa")))


def local(
    encoded,
    key_weight,
    value_weight,
    queries,
    key_len,
    retr_query,
    passage_ids,
    placement_perm,
    pool_in,
    pool_pre,
    pool_len,
    up_weight,
    up_bias,
    down_weight,
    norm_gain,
):
    q_here, p_here, tokens, width = encoded.shape
    pb_count = lax.axis_size("pb")
    pa_count = lax.axis_size("pa")
    ma_count = lax.axis_size("ma")
    pb_at = lax.axis_index("pb")
    pa_at = lax.axis_index("pa")
    ma_at = lax.axis_index("ma")
    heads_here = HEADS // ma_count
    cols_here = key_weight.shape[1]
    depth = key_weight.shape[0]
    token_rows = encoded.reshape(p_here * tokens, width)

    order = jnp.array(ring_order(pa_count), jnp.int32)
    place = jnp.argmax(order == pa_at).astype(jnp.int32)

    def owner_of(step):
        return order[(place - step + pa_count) % pa_count]

    def placed(step, parts):
        return [(owner_of(step) * pb_count + (pb_at ^ q), part) for q, part in enumerate(parts)]

    positions = jnp.arange(tokens, dtype=jnp.int32)
    grouped = pa_count <= RING_MOST
    rows = DR // (pb_count * pa_count)
    ff_here = up_weight.shape[1]
    ma_flip = [(i, ma_count - 1 - i) for i in range(ma_count)]
    blocks = cols_here // COLUMNS
    in_block = COLUMNS // HDIM
    pairs = ANS * heads_here
    same = jnp.eye(in_block, dtype=jnp.bfloat16)
    query_blocks = jnp.einsum(
        "abgj,gh->gjbha", queries[0].reshape(ANS, blocks, in_block, HDIM), same
    ).reshape(COLUMNS, pairs)
    valid = (positions[None, :] < key_len[0][:, None]).astype(jnp.float32).reshape(-1, 1)
    valid = jnp.broadcast_to(valid, (p_here * tokens, pairs // blocks))
    if grouped:
        first = ma_at == 0
        mine = jnp.where(first, pool_in[0], pool_pre[0])
        mine = jnp.concatenate([mine, jnp.full((LENGTH_ROWS, DR), pool_len[0], jnp.bfloat16)], axis=0)

        ring = []
        for weight in (key_weight, value_weight):
            piece = quarter_of(weight)
            if ring:
                piece = after(piece, ring[-1])
            for _ in range(pa_count - 1):
                if len(ring) == 2 * pa_count - 3:
                    mine = after(mine, piece)
                    mine = [mine] + [
                        lax.ppermute(mine, "pa", [((i + s) % pa_count, i) for i in range(pa_count)])
                        for s in range(1, pa_count)
                    ]
                piece = ring_step(piece)
                ring.append(piece)
        plane = PlaneGathers(ring)
        while (pa_count % 2, "b", pa_count - 2) not in plane.got:
            plane.turn()
        key_slices = [plane.slice(r) for r in range(pa_count - 1)]
    else:
        whole = lax.all_gather(key_weight, "pa", axis=0, tiled=True)
        weights, stats = scores_of(None, token_rows, [(0, whole)], query_blocks, valid, p_here)
    if grouped:
        keys = running(None, token_rows, [(pa_at, key_weight)] + placed(1, key_slices[0]))
        keys = running(keys, token_rows, placed(2, key_slices[1]))
        rest = [pair for step in range(3, pa_count) for pair in placed(step, key_slices[step - 1])]
        weights, stats = scores_of(keys, token_rows, rest, query_blocks, valid, p_here)
    if grouped:
        mine = after(jnp.stack(mine), stats)
        other = lax.ppermute(mine, "ma", ma_flip)
        inputs_in = ma_at
    else:
        lengths = jnp.full((1, LENGTH_ROWS, DR), pool_len[0], jnp.bfloat16)
        mine = jnp.concatenate([pool_in, lengths], axis=1)
        other = jnp.concatenate([pool_pre, lengths], axis=1)
        inputs_in = 0
    count = mine.shape[0]

    block = jnp.arange(DR, dtype=jnp.int32)
    if grouped:
        kept = jnp.arange(pb_count * rows, dtype=jnp.int32)
        kept = (kept // rows * pa_count + pa_at) * rows + kept % rows
    else:
        kept = block
    chosen = (block[:, None] == kept[None, :]).astype(jnp.bfloat16)
    grad_up, grad_down, sims, dpre, dup_b = backward(
        jnp.asarray(inputs_in, jnp.int32).reshape(1),
        mine,
        other,
        up_weight,
        up_bias[None],
        down_weight,
        norm_gain[None],
        retr_query,
        chosen,
    )
    sims = sims[:, 0, 0]
    if grouped:
        plane.turn()
        plane.turn()
        plane.turn()
        early = set(plane.got)
        while plane.turn(grad_up, grad_down):
            pass
    partial_back = jnp.einsum("rf,df->rd", dup_b, up_weight, preferred_element_type=jnp.float32)
    grad_in = dpre + partial_back + lax.ppermute(partial_back, "ma", ma_flip)

    if grouped:
        stats = jnp.stack(
            [stats]
            + [
                lax.ppermute(stats, "pa", [((i + s) % pa_count, i) for i in range(pa_count)])
                for s in range(1, pa_count)
            ]
        )
    else:
        stats = jnp.roll(lax.all_gather(stats, "pa", axis=0, tiled=False), -pa_at, axis=0)
    best = jnp.max(stats[:, 0], axis=0)
    factor = jnp.exp(stats[:, 0] - best[None])
    sums_all = stats[:, 1:] * factor[:, None]
    totals = jnp.sum(sums_all, axis=(0, 1))
    mass = jnp.sum(sums_all / totals, axis=-1) / (ANS * HEADS)
    mass = mass + lax.ppermute(mass, "ma", ma_flip)
    mass = jnp.roll(mass, pa_at, axis=0).reshape(pa_count * p_here)
    if grouped:
        sims = jnp.roll(sims, pa_at)
    else:
        sims = lax.all_gather(sims, "pa", axis=0, tiled=True)
    where_at = placement_perm[0][passage_ids[0]]
    p_ret = jax.nn.softmax(sims[where_at])
    coef = loss_scale * (p_ret - mass)
    held = (jnp.arange(count, dtype=jnp.int32) + pa_at) % pa_count
    scalars = jnp.sum(jnp.where(where_at[None, :] == held[:, None], coef[None, :], 0.0), axis=1)

    pool_grad = (grad_in * scalars[0]).astype(jnp.bfloat16)[None]

    def scatter_sum(grads, bits):
        total = grads[0] * scalars[0]
        for k in range(1, count):
            total = total + grads[k] * scalars[k]
        if not grouped:
            total = jnp.transpose(total.reshape(pb_count, pa_count, rows, ff_here), (1, 0, 2, 3))
            total = lax.psum_scatter(total, "pa", scatter_dimension=0, tiled=False)
        parts = total.reshape(pb_count, rows, ff_here)
        for bit in bits:
            split = parts.reshape((-1, 2, bit if parts.shape[0] == pb_count else 1) + parts.shape[1:])
            side = (pb_at // bit) % 2
            keep = lax.dynamic_index_in_dim(split, side, 1, keepdims=False)
            give = lax.dynamic_index_in_dim(split, 1 - side, 1, keepdims=False)
            got = flip(give.astype(jnp.bfloat16), bit)
            parts = (keep + got.astype(jnp.float32)).reshape((-1,) + parts.shape[1:])
        return parts[0]

    up_grad = scatter_sum(grad_up, (1, 2))
    down_grad = scatter_sum(grad_down, (2, 1))

    if grouped:
        ready, late = [(pa_at, value_weight)], []
        for r in range(pa_count - 1, 2 * (pa_count - 1)):
            step = r - pa_count + 2
            keys_of = [None, (0, "a", r), (1, "a", r), (r % 2, "b", r)]
            for key, pair in zip(keys_of, placed(step, plane.slice(r))):
                (ready if key is None or key in early else late).append(pair)
        values = running(None, after(token_rows, grad_up, grad_down), ready)
        last_values = (after(values, pool_grad), token_rows, late)
    else:
        whole = lax.all_gather(value_weight, "pa", axis=0, tiled=True)
        last_values = (None, token_rows, [(0, whole)])
    summed = summed_of(*last_values, weights, (factor[0] / totals)[None])
    if grouped:
        step = 1
        while step < pa_count:
            sent = summed.astype(jnp.bfloat16)
            got = lax.ppermute(sent, "pa", [(i, i ^ step) for i in range(pa_count)])
            summed = sent.astype(jnp.float32) + got.astype(jnp.float32)
            step *= 2
    else:
        summed = lax.psum(summed, "pa")
    attn_out = summed.astype(jnp.bfloat16).reshape(q_here, ANS, cols_here)
    return (attn_out, pool_grad, up_grad, down_grad)


def solution(mesh):
    return jax.shard_map(
        local,
        mesh=mesh,
        in_specs=(
            P("pb", "pa", None, None),
            P("pa", "ma"),
            P("pa", "ma"),
            P("pb", None, "ma"),
            P("pb", "pa"),
            P("pb", None),
            P("pb", None),
            P("pb", None),
            P(("pb", "pa"), None, None),
            P(("pb", "pa"), None, None),
            P(("pb", "pa")),
            P(None, "ma"),
            P("ma"),
            P(None, "ma"),
            P(),
        ),
        out_specs=(
            P("pb", None, "ma"),
            P(("pb", "pa"), None, None),
            P(("pb", "pa"), "ma"),
            P(("pb", "pa"), "ma"),
        ),
        check_vma=False,
    )
```

```python
import jax
import jax.numpy as jnp
from jax import lax
from jax.experimental import pallas as pl
from jax.experimental.pallas import tpu as pltpu
from jax.sharding import PartitionSpec as P

HEADS = 32
HDIM = 64
ANS = 32
DR = 768


RING_MOST = 4


loss_scale = 16384.0
highest = lax.Precision.HIGHEST


def ring_order(count):
    return list(range(0, count, 2)) + [i for i in range(count - 1, 0, -1) if i % 2]


def ring_next(count):
    order = ring_order(count)
    return [(order[i], order[(i + 1) % count]) for i in range(count)]


def flip(values, bit):
    count = lax.axis_size("pb")
    return lax.ppermute(values, "pb", [(i, i ^ bit) for i in range(count)])


def after(value, *others):
    return lax.optimization_barrier((value,) + others)[0]


def plane_slots(count):
    if count == 6:
        x = ["a0", "a1", "b0", "a2", "b2", "a3", "a4", "a5", "b4"]
        y = ["a0", "a1", "a2", "b1", "a3", "a4", "a5", "b3", "b5"]
    else:
        x, y = [], []
        for r in range(count):
            x.append(f"a{r}")
            y.append(f"a{r}")
            (x, y)[r % 2].append(f"b{r}")
    return [[(slot[0], int(slot[1:])) for slot in link] for link in (x, y)]


class PlaneGathers:
    def __init__(self, ring):
        self.ring = ring
        self.left = plane_slots(len(ring))
        self.got = {}
        self.turns = []

    def turn(self, *others):
        now = []
        for link in (0, 1):
            if not self.left[link]:
                continue
            kind, r = self.left[link][0]
            if kind == "b" and (1 - link, "a", r) not in self.got:
                continue
            self.left[link].pop(0)
            data = self.ring[r] if kind == "a" else self.got[(1 - link, "a", r)]
            before = (self.turns[-2] if len(self.turns) > 1 else []) + list(others)
            if before:
                data = after(data, *before)
            now.append((link, kind, r, flip(data, 1 + link)))
        for link, kind, r, value in now:
            self.got[(link, kind, r)] = value
        self.turns.append([value for _, _, _, value in now])
        return bool(self.left[0] or self.left[1])

    def slice(self, r):
        return [self.ring[r], self.got[(0, "a", r)], self.got[(1, "a", r)], self.got[(r % 2, "b", r)]]


LENGTH_ROWS = 16
COLUMNS = 256


def accumulate(refs, has_total, count):
    total = refs[0][...] if has_total else None
    at = 1 if has_total else 0
    for _ in range(count):
        term = jnp.dot(refs[at][...], refs[at + 1][...], preferred_element_type=jnp.float32)
        total = term if total is None else total + term
        at += 2
    return total, refs[at:]


def two_terms(values):
    high = values.astype(jnp.bfloat16)
    return high, (values - high.astype(jnp.float32)).astype(jnp.bfloat16)


def projection(total, rows, pairs, finish, extra, extra_specs, out_shape, out_specs):
    arrays = [] if total is None else [total]
    specs = [] if total is None else [pl.BlockSpec((total.shape[0], COLUMNS), lambda i, at: (0, i))]
    flops = 0
    for n, (_, part) in enumerate(pairs):
        arrays += [rows, part]
        specs += [
            pl.BlockSpec((rows.shape[0], part.shape[0]), lambda i, at, n=n: (0, at[n])),
            pl.BlockSpec((part.shape[0], COLUMNS), lambda i, at: (0, i)),
        ]
        flops += 2 * rows.shape[0] * part.shape[0] * part.shape[1]
    places = jnp.stack([jnp.asarray(place, jnp.int32) for place, _ in pairs])

    def kernel(places_ref, *refs):
        value, rest = accumulate(refs, total is not None, len(pairs))
        finish(value, *rest)

    return pl.pallas_call(
        kernel,
        grid_spec=pltpu.PrefetchScalarGridSpec(
            num_scalar_prefetch=1,
            grid=(pairs[0][1].shape[1] // COLUMNS,),
            in_specs=specs + list(extra_specs),
            out_specs=out_specs,
        ),
        out_shape=out_shape,
        compiler_params=pltpu.CompilerParams(vmem_limit_bytes=32 << 20),
        cost_estimate=pl.CostEstimate(flops=flops, bytes_accessed=8 << 20, transcendentals=0),
    )(places, *arrays, *extra)


def store(value, out_ref):
    out_ref[...] = value


def running(total, rows, pairs):
    tokens, columns = rows.shape[0], pairs[0][1].shape[1]
    return projection(
        total,
        rows,
        pairs,
        store,
        (),
        (),
        jax.ShapeDtypeStruct((tokens, columns), jnp.float32),
        pl.BlockSpec((tokens, COLUMNS), lambda i, at: (0, i)),
    )


def scores_of(total, rows, pairs, query_blocks, valid, p_here):
    tokens = rows.shape[0]
    queries = query_blocks.shape[1]
    blocks = pairs[0][1].shape[1] // COLUMNS
    each = tokens // p_here

    def finish(keys, query_ref, valid_ref, weight_ref, stat_ref):
        high, low = two_terms(keys)
        query = query_ref[...]
        scores = jnp.dot(high, query, preferred_element_type=jnp.float32)
        scores = scores + jnp.dot(low, query, preferred_element_type=jnp.float32)
        alive = valid_ref[...] > 0.0
        scores = jnp.where(alive, scores, -1e30)
        top = jnp.max(scores, axis=0, keepdims=True)
        weights = jnp.where(alive, jnp.exp(scores - top), 0.0)
        weight_ref[...] = weights
        lines = [top] + [
            jnp.sum(weights[p * each : (p + 1) * each], axis=0, keepdims=True) for p in range(p_here)
        ]
        for i, row in enumerate(lines):
            stat_ref[i : i + 1, :] = row

    wide = queries // blocks
    return projection(
        total,
        rows,
        pairs,
        finish,
        (query_blocks, valid),
        (
            pl.BlockSpec((COLUMNS, wide), lambda i, at: (0, i)),
            pl.BlockSpec((tokens, wide), lambda i, at: (0, 0)),
        ),
        (
            jax.ShapeDtypeStruct((tokens, queries), jnp.float32),
            jax.ShapeDtypeStruct((1 + p_here, queries), jnp.float32),
        ),
        (
            pl.BlockSpec((tokens, wide), lambda i, at: (0, i)),
            pl.BlockSpec((1 + p_here, wide), lambda i, at: (0, i)),
        ),
    )


def summed_of(total, rows, pairs, weights, ratio):
    tokens, queries = weights.shape
    columns = pairs[0][1].shape[1]
    blocks = columns // COLUMNS
    wide = queries // blocks

    def finish(values, weight_ref, ratio_ref, out_ref):
        high, low = two_terms(values)
        w_high, w_low = two_terms(weight_ref[...] * ratio_ref[...])
        over = (((0,), (0,)), ((), ()))
        full = lax.dot_general(w_high, high, over, preferred_element_type=jnp.float32)
        full = full + lax.dot_general(w_high, low, over, preferred_element_type=jnp.float32)
        full = full + lax.dot_general(w_low, high, over, preferred_element_type=jnp.float32)
        head = lax.broadcasted_iota(jnp.int32, (ANS, COLUMNS), 1) // HDIM
        out = jnp.zeros((ANS, COLUMNS), jnp.float32)
        for h in range(COLUMNS // HDIM):
            out = jnp.where(head == h, full[h * ANS : (h + 1) * ANS], out)
        out_ref[...] = out

    return projection(
        total,
        rows,
        pairs,
        finish,
        (weights, ratio),
        (
            pl.BlockSpec((tokens, wide), lambda i, at: (0, i)),
            pl.BlockSpec((1, wide), lambda i, at: (0, i)),
        ),
        jax.ShapeDtypeStruct((ANS, columns), jnp.float32),
        pl.BlockSpec((ANS, COLUMNS), lambda i, at: (0, i)),
    )


def backward_kernel(
    place_ref, mine_ref, other_ref, up_ref, bias_ref, down_ref, gain_ref, query_ref, chosen_ref,
    grad_up_ref, grad_down_ref, sim_ref, dpre_ref, dup_ref,
):
    tokens = mine_ref.shape[1] - LENGTH_ROWS
    mine = mine_ref[0].astype(jnp.float32)
    other = other_ref[0].astype(jnp.float32)
    swap = place_ref[0] != 0
    inputs = jnp.where(swap, other, mine)[:tokens].astype(jnp.bfloat16)
    pre = jnp.where(swap, mine, other)[:tokens]
    length = mine[tokens : tokens + 1, 0:1]
    gain, query = gain_ref[...], query_ref[...]
    centre = pre - jnp.mean(pre, axis=-1, keepdims=True)
    spread = jnp.mean(centre * centre, axis=-1, keepdims=True)
    inverse = 1.0 / jnp.sqrt(spread + 1e-05)
    normed = centre * inverse
    position = lax.broadcasted_iota(jnp.int32, (tokens, 1), 0).astype(jnp.float32)
    live = (position < length).astype(jnp.float32)
    embed = jnp.sum(normed * gain * live, axis=0, keepdims=True) / length
    sim = jnp.sum(embed * query, axis=-1, keepdims=True)
    sim_ref[0] = jnp.broadcast_to(sim, sim_ref.shape[1:])
    dnorm = query * live * gain / length
    dpre = (
        dnorm
        - jnp.mean(dnorm, axis=-1, keepdims=True)
        - normed * jnp.mean(dnorm * normed, axis=-1, keepdims=True)
    ) * inverse
    dpre_b = dpre.astype(jnp.bfloat16)
    chosen = chosen_ref[...]
    inputs_part = jnp.dot(inputs, chosen, preferred_element_type=jnp.float32).astype(jnp.bfloat16)
    dpre_part = jnp.dot(dpre_b, chosen, preferred_element_type=jnp.float32).astype(jnp.bfloat16)
    over = (((0,), (0,)), ((), ()))
    wide = 512
    for start in range(0, up_ref.shape[1], wide):
        cols = slice(start, start + wide)
        upper = jnp.dot(inputs, up_ref[:, cols], preferred_element_type=jnp.float32) + bias_ref[:, cols]
        dact = jnp.dot(dpre_b, down_ref[:, cols], preferred_element_type=jnp.float32)
        below = 0.5 * (1.0 + lax.erf(upper * 0.7071067811865476))
        act_b = (upper * below).astype(jnp.bfloat16)
        slope = below + upper * jnp.exp(-0.5 * upper * upper) * 0.3989422804014327
        dup_b = (dact * slope).astype(jnp.bfloat16)
        grad_up_ref[0, :, cols] = lax.dot_general(inputs_part, dup_b, over, preferred_element_type=jnp.float32)
        grad_down_ref[0, :, cols] = lax.dot_general(dpre_part, act_b, over, preferred_element_type=jnp.float32)

        @pl.when(pl.program_id(0) == 0)
        def _():
            dup_ref[:, cols] = dup_b

    @pl.when(pl.program_id(0) == 0)
    def _():
        dpre_ref[...] = dpre


def backward(place, mine, other, up_weight, up_bias, down_weight, gain, query, chosen):
    count, padded, width = mine.shape
    tokens = padded - LENGTH_ROWS
    hidden, part = up_weight.shape[1], chosen.shape[1]
    whole = lambda array: pl.BlockSpec(array.shape, lambda k, at: (0, 0))
    one = lambda *shape: pl.BlockSpec((1,) + shape, lambda k, at: (k, 0, 0))
    fixed = lambda *shape: pl.BlockSpec(shape, lambda k, at: (0, 0))
    flops = 4 * count * tokens * hidden * (width + part)
    return pl.pallas_call(
        backward_kernel,
        grid_spec=pltpu.PrefetchScalarGridSpec(
            num_scalar_prefetch=1,
            grid=(count,),
            in_specs=[one(padded, width), one(padded, width)]
            + [whole(a) for a in (up_weight, up_bias, down_weight, gain, query, chosen)],
            out_specs=[one(part, hidden), one(part, hidden), one(1, 128), fixed(tokens, width), fixed(tokens, hidden)],
        ),
        out_shape=[
            jax.ShapeDtypeStruct((count, part, hidden), jnp.float32),
            jax.ShapeDtypeStruct((count, part, hidden), jnp.float32),
            jax.ShapeDtypeStruct((count, 1, 128), jnp.float32),
            jax.ShapeDtypeStruct((tokens, width), jnp.float32),
            jax.ShapeDtypeStruct((tokens, hidden), jnp.bfloat16),
        ],
        compiler_params=pltpu.CompilerParams(vmem_limit_bytes=32 << 20),
        cost_estimate=pl.CostEstimate(flops=flops, bytes_accessed=24 << 20, transcendentals=2 * count * tokens * hidden),
    )(place, mine, other, up_weight, up_bias, down_weight, gain, query, chosen)


def quarter_of(weight):
    quarter = weight.shape[0] // lax.axis_size("pb")
    return lax.dynamic_slice_in_dim(weight, lax.axis_index("pb") * quarter, quarter, 0)


def ring_step(piece):
    return lax.ppermute(piece, "pa", ring_next(lax.axis_size("pa")))


def local(
    encoded,
    key_weight,
    value_weight,
    queries,
    key_len,
    retr_query,
    passage_ids,
    placement_perm,
    pool_in,
    pool_pre,
    pool_len,
    up_weight,
    up_bias,
    down_weight,
    norm_gain,
):
    q_here, p_here, tokens, width = encoded.shape
    pb_count = lax.axis_size("pb")
    pa_count = lax.axis_size("pa")
    ma_count = lax.axis_size("ma")
    pb_at = lax.axis_index("pb")
    pa_at = lax.axis_index("pa")
    ma_at = lax.axis_index("ma")
    heads_here = HEADS // ma_count
    cols_here = key_weight.shape[1]
    depth = key_weight.shape[0]
    token_rows = encoded.reshape(p_here * tokens, width)

    order = jnp.array(ring_order(pa_count), jnp.int32)
    place = jnp.argmax(order == pa_at).astype(jnp.int32)

    def owner_of(step):
        return order[(place - step + pa_count) % pa_count]

    def placed(step, parts):
        return [(owner_of(step) * pb_count + (pb_at ^ q), part) for q, part in enumerate(parts)]

    positions = jnp.arange(tokens, dtype=jnp.int32)
    grouped = pa_count <= RING_MOST
    rows = DR // (pb_count * pa_count)
    ff_here = up_weight.shape[1]
    ma_flip = [(i, ma_count - 1 - i) for i in range(ma_count)]
    blocks = cols_here // COLUMNS
    in_block = COLUMNS // HDIM
    pairs = ANS * heads_here
    same = jnp.eye(in_block, dtype=jnp.bfloat16)
    query_blocks = jnp.einsum(
        "abgj,gh->gjbha", queries[0].reshape(ANS, blocks, in_block, HDIM), same
    ).reshape(COLUMNS, pairs)
    valid = (positions[None, :] < key_len[0][:, None]).astype(jnp.float32).reshape(-1, 1)
    valid = jnp.broadcast_to(valid, (p_here * tokens, pairs // blocks))
    if grouped:
        first = ma_at == 0
        mine = jnp.where(first, pool_in[0], pool_pre[0])
        mine = jnp.concatenate([mine, jnp.full((LENGTH_ROWS, DR), pool_len[0], jnp.bfloat16)], axis=0)

        ring = []
        for weight in (key_weight, value_weight):
            piece = quarter_of(weight)
            if ring:
                piece = after(piece, ring[-1])
            for _ in range(pa_count - 1):
                if len(ring) == 2 * pa_count - 3:
                    mine = after(mine, piece)
                    mine = [mine] + [
                        lax.ppermute(mine, "pa", [((i + s) % pa_count, i) for i in range(pa_count)])
                        for s in range(1, pa_count)
                    ]
                piece = ring_step(piece)
                ring.append(piece)
        plane = PlaneGathers(ring)
        while (pa_count % 2, "b", pa_count - 2) not in plane.got:
            plane.turn()
        key_slices = [plane.slice(r) for r in range(pa_count - 1)]
    else:
        whole = lax.all_gather(key_weight, "pa", axis=0, tiled=True)
        weights, stats = scores_of(None, token_rows, [(0, whole)], query_blocks, valid, p_here)
    if grouped:
        keys = running(None, token_rows, [(pa_at, key_weight)] + placed(1, key_slices[0]))
        keys = running(keys, token_rows, placed(2, key_slices[1]))
        rest = [pair for step in range(3, pa_count) for pair in placed(step, key_slices[step - 1])]
        weights, stats = scores_of(keys, token_rows, rest, query_blocks, valid, p_here)
    if grouped:
        mine = after(jnp.stack(mine), stats)
        other = lax.ppermute(mine, "ma", ma_flip)
        inputs_in = ma_at
    else:
        lengths = jnp.full((1, LENGTH_ROWS, DR), pool_len[0], jnp.bfloat16)
        mine = jnp.concatenate([pool_in, lengths], axis=1)
        other = jnp.concatenate([pool_pre, lengths], axis=1)
        inputs_in = 0
    count = mine.shape[0]

    block = jnp.arange(DR, dtype=jnp.int32)
    if grouped:
        kept = jnp.arange(pb_count * rows, dtype=jnp.int32)
        kept = (kept // rows * pa_count + pa_at) * rows + kept % rows
    else:
        kept = block
    chosen = (block[:, None] == kept[None, :]).astype(jnp.bfloat16)
    grad_up, grad_down, sims, dpre, dup_b = backward(
        jnp.asarray(inputs_in, jnp.int32).reshape(1),
        mine,
        other,
        up_weight,
        up_bias[None],
        down_weight,
        norm_gain[None],
        retr_query,
        chosen,
    )
    sims = sims[:, 0, 0]
    if grouped:
        plane.turn()
        plane.turn()
        plane.turn()
        early = set(plane.got)
        while plane.turn(grad_up, grad_down):
            pass
    partial_back = jnp.einsum("rf,df->rd", dup_b, up_weight, preferred_element_type=jnp.float32)
    grad_in = dpre + partial_back + lax.ppermute(partial_back, "ma", ma_flip)

    if grouped:
        stats = jnp.stack(
            [stats]
            + [
                lax.ppermute(stats, "pa", [((i + s) % pa_count, i) for i in range(pa_count)])
                for s in range(1, pa_count)
            ]
        )
    else:
        stats = jnp.roll(lax.all_gather(stats, "pa", axis=0, tiled=False), -pa_at, axis=0)
    best = jnp.max(stats[:, 0], axis=0)
    factor = jnp.exp(stats[:, 0] - best[None])
    sums_all = stats[:, 1:] * factor[:, None]
    totals = jnp.sum(sums_all, axis=(0, 1))
    mass = jnp.sum(sums_all / totals, axis=-1) / (ANS * HEADS)
    mass = mass + lax.ppermute(mass, "ma", ma_flip)
    mass = jnp.roll(mass, pa_at, axis=0).reshape(pa_count * p_here)
    if grouped:
        sims = jnp.roll(sims, pa_at)
    else:
        sims = lax.all_gather(sims, "pa", axis=0, tiled=True)
    where_at = placement_perm[0][passage_ids[0]]
    p_ret = jax.nn.softmax(sims[where_at])
    coef = loss_scale * (p_ret - mass)
    held = (jnp.arange(count, dtype=jnp.int32) + pa_at) % pa_count
    scalars = jnp.sum(jnp.where(where_at[None, :] == held[:, None], coef[None, :], 0.0), axis=1)

    pool_grad = (grad_in * scalars[0]).astype(jnp.bfloat16)[None]

    def scatter_sum(grads, bits):
        total = grads[0] * scalars[0]
        for k in range(1, count):
            total = total + grads[k] * scalars[k]
        if not grouped:
            total = jnp.transpose(total.reshape(pb_count, pa_count, rows, ff_here), (1, 0, 2, 3))
            total = lax.psum_scatter(total, "pa", scatter_dimension=0, tiled=False)
        parts = total.reshape(pb_count, rows, ff_here)
        for bit in bits:
            split = parts.reshape((-1, 2, bit if parts.shape[0] == pb_count else 1) + parts.shape[1:])
            side = (pb_at // bit) % 2
            keep = lax.dynamic_index_in_dim(split, side, 1, keepdims=False)
            give = lax.dynamic_index_in_dim(split, 1 - side, 1, keepdims=False)
            got = flip(give.astype(jnp.bfloat16), bit)
            parts = (keep + got.astype(jnp.float32)).reshape((-1,) + parts.shape[1:])
        return parts[0]

    up_grad = scatter_sum(grad_up, (1, 2))
    down_grad = scatter_sum(grad_down, (2, 1))

    if grouped:
        ready, late = [(pa_at, value_weight)], []
        for r in range(pa_count - 1, 2 * (pa_count - 1)):
            step = r - pa_count + 2
            keys_of = [None, (0, "a", r), (1, "a", r), (r % 2, "b", r)]
            for key, pair in zip(keys_of, placed(step, plane.slice(r))):
                (ready if key is None or key in early else late).append(pair)
        values = running(None, after(token_rows, grad_up, grad_down), ready)
        last_values = (after(values, pool_grad), token_rows, late)
    else:
        whole = lax.all_gather(value_weight, "pa", axis=0, tiled=True)
        last_values = (None, token_rows, [(0, whole)])
    summed = summed_of(*last_values, weights, (factor[0] / totals)[None])
    if grouped:
        step = 1
        while step < pa_count:
            sent = summed.astype(jnp.bfloat16)
            got = lax.ppermute(sent, "pa", [(i, i ^ step) for i in range(pa_count)])
            summed = sent.astype(jnp.float32) + got.astype(jnp.float32)
            step *= 2
    else:
        summed = lax.psum(summed, "pa")
    attn_out = summed.astype(jnp.bfloat16).reshape(q_here, ANS, cols_here)
    return (attn_out, pool_grad, up_grad, down_grad)


def solution(mesh):
    return jax.shard_map(
        local,
        mesh=mesh,
        in_specs=(
            P("pb", "pa", None, None),
            P("pa", "ma"),
            P("pa", "ma"),
            P("pb", None, "ma"),
            P("pb", "pa"),
            P("pb", None),
            P("pb", None),
            P("pb", None),
            P(("pb", "pa"), None, None),
            P(("pb", "pa"), None, None),
            P(("pb", "pa")),
            P(None, "ma"),
            P("ma"),
            P(None, "ma"),
            P(),
        ),
        out_specs=(
            P("pb", None, "ma"),
            P(("pb", "pa"), None, None),
            P(("pb", "pa"), "ma"),
            P(("pb", "pa"), "ma"),
        ),
        check_vma=False,
    )
```
